1024 devices in a mesh: rep: 16 (over x, core), fsdp: 64 (over z, y).
Axes of the slice: x: 8, y: 8, z: 8, core: 2. Of those that a mesh axis runs over, the one named last changes fastest.
Arguments:
- deltas: bfloat16 [16, 4096, 8192], P('rep', None, 'fsdp'), may hold values from -6 to 6
- sign_bits: int32 [16, 8192], replicated, may hold values from 0 to 1
- kept_tiles: int32 [16, 32], replicated, may hold values from 0 to 63, as said below
- kept_count: int32 [16], replicated, may hold values from 8 to 32, as said below
- params: float32 [4096, 8192], P(('fsdp', 'rep')), may hold values from -6 to 6
- momentum: float32 [4096, 8192], P(('fsdp', 'rep')), may hold values from -4 to 4
Outputs:
- new_params: float32 [4096, 8192], P(('fsdp', 'rep'))
- new_momentum: float32 [4096, 8192], P(('fsdp', 'rep'))
- working: bfloat16 [4096, 8192], P(None, 'fsdp')
The draws below stay inside these ranges and needn't reach their ends.
Inputs may be any that keep to these rules, and one draw needn't show every extreme that they name: `kept_count`: how many tiles each replica keeps; some replica keeps exactly 32. `kept_tiles`: each row holds distinct tile numbers; the first kept_count[r] entries of row r name the tiles replica r keeps, the rest are unused.
All inputs are finite; a program needn't handle non-finite values.
Results may differ from the reference program's by a relative error of at most 0.0034.
Values may be sent and summed in bfloat16 or wider, within the bound.
A program may use at most 32 MiB of HBM per device.

```python
import math
import jax
import jax.numpy as jnp
from jax import lax

D = 4096
F = 8192
BLOCK = 1024
TILE = 128
TILES = 64
MOST = 32
REPLICAS = 16


def tile_plan(key):
    count_key, pick_key, order_key = jax.random.split(key, 3)
    counts = jax.random.randint(count_key, (REPLICAS,), MOST // 4, MOST + 1)
    chosen = jax.random.randint(pick_key, (), 0, REPLICAS)
    counts = jnp.where(jnp.arange(REPLICAS) == chosen, MOST, counts).astype(jnp.int32)
    subkeys = jax.random.split(order_key, REPLICAS)
    orders = jax.vmap(lambda subkey: jax.random.permutation(subkey, TILES))(subkeys)
    return (counts, orders[:, :MOST].astype(jnp.int32))


def draw_kept_tiles(key, part):
    plan = tile_plan(key)
    return plan[1]


def draw_kept_count(key, part):
    plan = tile_plan(key)
    return plan[0]


def set_ends(drawn, rng, smallest, top_value):
    longest = drawn.shape.index(max(drawn.shape))
    spots = []
    for shift in (0, 1):
        where = [jax.random.randint(jax.random.fold_in(rng, axis), (), 0, length) for axis, length in enumerate(drawn.shape)]
        where[longest] = (where[longest] + shift) % drawn.shape[longest]
        spots.append(tuple(where))
    return drawn.at[spots[0]].set(smallest).at[spots[1]].set(top_value)


def block_levels(own_key, dims, cuts, smallest, top_value):
    factor_of = 1.0
    for dim, shards_of in cuts:
        draws = jax.random.uniform(jax.random.fold_in(jax.random.fold_in(own_key, 6), dim), (shards_of,), jnp.float32, smallest / len(cuts), top_value / len(cuts))
        factor_of = factor_of * jnp.repeat(jnp.exp(draws), dims[dim] // shards_of).reshape((-1,) + (1,) * (len(dims) - 1 - dim))
    return factor_of


def centred(key, dims, width, bound, cuts=(), held_as=jnp.bfloat16):
    drawn = jax.random.normal(key, dims, jnp.float32) * width
    if len(cuts) > 0:
        drawn = block_levels(key, dims, cuts, -0.22, 0.18) * drawn
    return jnp.clip(drawn, min=-bound, max=bound).astype(held_as)


def setup_inputs(seed: int = 0) -> dict:
    keys = jax.random.split(jax.random.key(seed), 7)
    deltas = centred(keys[0], (REPLICAS, D, F), 1.0, 6.0, ((0, 16), (2, 64)))
    sign_bits = set_ends(jax.random.randint(keys[1], (REPLICAS, F), 0, 2), jax.random.fold_in(keys[1], 1), 0, 1).astype(jnp.int32)
    kept_tiles = draw_kept_tiles(jax.random.fold_in(keys[6], 71), 0)
    kept_count = draw_kept_count(jax.random.fold_in(keys[6], 71), 0)
    params = centred(keys[4], (D, F), 1.0, 6.0, ((0, 1024),), jnp.float32)
    momentum = centred(keys[5], (D, F), 0.3, 4.0, ((0, 1024),), jnp.float32)
    return dict(deltas=deltas, sign_bits=sign_bits, kept_tiles=kept_tiles, kept_count=kept_count, params=params, momentum=momentum)


def sylvester_signs(order):
    indices = jnp.arange(order, dtype=jnp.int32)
    intersection = indices[:, None] & indices[None, :]
    parity = jnp.zeros((order, order), jnp.int32)
    for bit_number in range(order.bit_length() - 1):
        parity = parity + (intersection >> bit_number & 1)
    return jnp.where(parity % 2 == 0, 1.0, -1.0).astype(jnp.float32)

def reference(deltas, sign_bits, kept_tiles, kept_count, params, momentum):
    small_side = 2 ** ((BLOCK.bit_length() - 1) // 2)
    large_side = BLOCK // small_side
    left_signs = sylvester_signs(small_side)
    right_signs = sylvester_signs(large_side)
    tile_index = jnp.arange(TILES, dtype=jnp.int32)
    slot_index = jnp.arange(MOST, dtype=jnp.int32)

    def rotate(values):
        row_total = values.shape[0]
        shaped = values.reshape(row_total, F // BLOCK, small_side, large_side)
        first = jnp.einsum('rnab,ac->rncb', shaped, left_signs, precision=lax.Precision.HIGHEST)
        second = jnp.einsum('rncb,bd->rncd', first, right_signs, precision=lax.Precision.HIGHEST)
        return second.reshape(row_total, F) * (1.0 / math.sqrt(BLOCK))

    def add_one(total, pieces):
        delta_one, bits_one, list_one, count_one = pieces
        sign_row = (1 - 2 * bits_one).astype(jnp.float32)
        rotated = rotate(delta_one.astype(jnp.float32) * sign_row[None, :])
        live = slot_index < count_one
        mask_tiles = lax.optimization_barrier(jnp.sum(((list_one[:, None] == tile_index[None, :]) & live[:, None]).astype(jnp.float32), axis=0))
        factor = TILES / count_one.astype(jnp.float32)
        weights = mask_tiles * factor
        compressed = (rotated.reshape(D, TILES, TILE) * weights[None, :, None]).reshape(D, F).astype(jnp.bfloat16)
        decoded = rotate(compressed.astype(jnp.float32)) * sign_row[None, :]
        return (total + decoded, None)
    total, _ = lax.scan(add_one, jnp.zeros((D, F), jnp.float32), (deltas, sign_bits, kept_tiles, kept_count))
    outer_grad = total / REPLICAS
    new_momentum = 0.9 * momentum + outer_grad
    new_params = params - 0.7 * (outer_grad + 0.9 * new_momentum)
    return (new_params, new_momentum, new_params.astype(jnp.bfloat16))
```

```python
import jax
import jax.numpy as jnp
from jax import lax
from jax.experimental import pallas as pl
from jax.experimental.pallas import tpu as pltpu
from jax.sharding import PartitionSpec as P

MESH = pl.DeviceIdType.MESH
DMA = pltpu.SemaphoreType.DMA
CHUNKS = 4
NZ = 8 // CHUNKS
MOST = 32
F32 = jnp.float32
BF16 = jnp.bfloat16


def place():
    rep = lax.axis_index("rep")
    col = lax.axis_index("fsdp")
    return rep // 2, rep % 2, col % 8, col // 8


def at(x, c, y, z):
    return (2 * x + c, 8 * z + y)


def loop(low, high, body):
    def step(i, carry):
        body(i)
        return carry

    lax.fori_loop(low, high, step, jnp.int32(0))


def butterfly(v):
    for bit in (1, 2, 4):
        v = [v[i] + v[i | bit] if not i & bit else v[i ^ bit] - v[i] for i in range(8)]
    return v


def hadamard128():
    i = lax.broadcasted_iota(jnp.int32, (128, 128), 0)
    j = lax.broadcasted_iota(jnp.int32, (128, 128), 1)
    v = i & j
    v = v ^ (v >> 4)
    v = v ^ (v >> 2)
    v = v ^ (v >> 1)
    return (1 - 2 * (v & 1)).astype(F32).astype(BF16)


def kernel(
    deltas, bits, tiles, counts, params, momentum,
    new_params, new_momentum, out,
    a_buf, s_buf, r_buf, w_buf, e_buf, q_out, q_in, g_out, g_in, sign_in, signs, weights, p_in, m_in,
    a_ss, a_rs, r_ss, r_rs, w_ss, e_rs, ag_ss, ag_rs, f_ss, f_rs, q_ss, q_rs, g_ss, g_rs, l_sem,
):
    x, c, y, z = place()
    half = x // 4
    quarter = x % 4
    pair = quarter // 2

    loads = [
        pltpu.make_async_copy(bits.at[pl.ds(pl.multiple_of(x // 4 * 8, 8), 8), pl.ds(pl.multiple_of(z * 1024, 1024), 1024)], sign_in, l_sem.at[0]),
        pltpu.make_async_copy(params, p_in, l_sem.at[1]),
        pltpu.make_async_copy(momentum, m_in, l_sem.at[2]),
    ]
    for load in loads:
        load.start()

    barrier = pltpu.get_barrier_semaphore()

    def greet(device):
        pl.semaphore_signal(barrier, inc=1, device_id=device, device_id_type=MESH)

    def greet_y(i):
        p = (2 * y + c + i) % 16
        greet(at(x, p % 2, p // 2, z))

    def greet_x(i):
        greet(at((x + i) % 8, c, y, z))

    def greet_z(i):
        p = (z * 8 + quarter * 2 + c + i) % 64
        greet(at(4 * half + p % 8 // 2, p % 2, y, p // 8))

    loop(1, 16, greet_y)
    loop(1, 8, greet_x)
    loop(1, 64, greet_z)
    stays = ((4 * half + y % 4) == x) & ((y // 2) == quarter)
    for t in range(2):
        own = (4 * half + y % 4 == x) & (2 * quarter + t == y)

        @pl.when(jnp.logical_not(own))
        def _():
            greet(at(4 * half + y % 4, c, 2 * quarter + t, z))

        own_in = (4 * half + y // 2 == x) & (quarter + 4 * t == y)

        @pl.when(jnp.logical_not(own_in))
        def _():
            greet(at(4 * half + y // 2, c, quarter + 4 * t, z))

    pl.semaphore_wait(barrier, 15 + 7 + 63 + 4 - 2 * stays.astype(jnp.int32))

    def y_peer(i):
        k = 8 + (2 * (i % 2) - 1) * ((i + 1) // 2)
        p = (2 * y + c + k) % 16
        return p // 2, p % 2

    def y_copy(j, i):
        py, pc = y_peer(i)
        return pltpu.make_async_remote_copy(
            src_ref=deltas.at[pl.ds(NZ * j, NZ), py, :, pc],
            dst_ref=a_buf.at[j, y, c],
            send_sem=a_ss.at[j, i],
            recv_sem=a_rs.at[j],
            device_id=at(x, pc, py, z),
            device_id_type=MESH,
        )

    def send_y(j):
        loop(0, 15, lambda i: y_copy(j, i).start())
        pltpu.make_async_copy(deltas.at[pl.ds(NZ * j, NZ), y, :, c], a_buf.at[j, y, c], a_rs.at[j]).start()

    send_y(0)
    send_y(1)

    loads[1].wait()
    loads[2].wait()
    for n in range(32):
        both = [
            p_in[:, (2 * n + t) * 128 : (2 * n + t + 1) * 128] - 0.567 * m_in[:, (2 * n + t) * 128 : (2 * n + t + 1) * 128]
            for t in range(2)
        ]
        q_out[n // 4, n % 4] = jnp.concatenate(both, axis=0)

    def q_target(i):
        pz = (z + i // 4) % 8
        m = i % 4
        return pz, m, (4 * half + m == x) & (pair == c) & (pz == z)

    def q_copy(i):
        pz, m, _ = q_target(i)
        return pltpu.make_async_remote_copy(
            src_ref=q_out.at[pz, m],
            dst_ref=q_in.at[z, x % 2, c],
            send_sem=q_ss.at[i],
            recv_sem=q_rs,
            device_id=at(4 * half + m, pair, y, pz),
            device_id_type=MESH,
        )

    def q_send(i):
        pz, m, own = q_target(i)

        @pl.when(jnp.logical_not(own))
        def _():
            q_copy(i).start()

        @pl.when(own)
        def _():
            pltpu.make_async_copy(q_out.at[pz, m], q_in.at[z, x % 2, c], q_rs).start()

    def q_done(i):
        @pl.when(jnp.logical_not(q_target(i)[2]))
        def _():
            q_copy(i).wait_send()

    loop(0, 32, q_send)

    loads[0].wait()
    lane = lax.broadcasted_iota(jnp.int32, (8, MOST), 1)
    wanted = lax.broadcasted_iota(jnp.int32, (8, MOST), 0) + 8 * z
    for s in range(2):
        row = sign_in[pl.ds(2 * x % 8 + s, 1), :]
        for k in range(8):
            signs[s, k : k + 1, :] = (1 - 2 * row[:, k * 128 : (k + 1) * 128]).astype(F32)
        count = counts[2 * x + s]
        kept = (tiles[pl.ds(2 * x + s, 1), :] == wanted) & (lane < count)
        mask = jnp.sum(kept.astype(F32), axis=1, keepdims=True)
        factor = (64.0 / 32.0) / jnp.full((8, 128), count, jnp.int32).astype(F32)
        weights[s] = mask * factor

    h128 = hadamard128()

    def rotate(parts):
        stacked = jnp.concatenate([parts[k][s] for k in range(8) for s in range(2)], axis=0)
        full = jnp.dot(stacked, h128, preferred_element_type=F32)
        return [[full[(2 * k + s) * 32 : (2 * k + s + 1) * 32] for s in range(2)] for k in range(8)]

    def columns(lists, f):
        sides = [f(s, [lists[k][s] for k in range(8)]) for s in range(2)]
        return [[sides[s][k] for s in range(2)] for k in range(8)]

    def compute(j):
        def group(i):
            flipped = [
                [(a_buf[j, k, s, i].reshape(32, 128).astype(F32) * signs[s, k : k + 1, :]).astype(BF16) for s in range(2)]
                for k in range(8)
            ]

            def middle(s, v):
                v = butterfly(v)
                return [(v[k] * weights[s, k : k + 1, :]).astype(BF16) for k in range(8)]

            def last(s, v):
                v = butterfly(v)
                return [v[k] * (signs[s, k : k + 1, :] * (1.0 / 512.0)) for k in range(8)]

            back = columns(rotate(columns(rotate(flipped), middle)), last)
            for k in range(8):
                s_buf[j, k, i] = (back[k][0] + back[k][1]).astype(BF16).reshape(2, 16, 128)

        loop(0, NZ, group)

    def x_copy(j, i):
        px = (x + 4 + (2 * (i % 2) - 1) * ((i + 1) // 2)) % 8
        return pltpu.make_async_remote_copy(
            src_ref=s_buf.at[j, pl.ds(2 * (px % 4), 2), :, px // 4],
            dst_ref=r_buf.at[j, x],
            send_sem=r_ss.at[j, i],
            recv_sem=r_rs.at[j],
            device_id=at(px, c, y, z),
            device_id_type=MESH,
        )

    def send_x(j):
        loop(0, 7, lambda i: x_copy(j, i).start())
        pltpu.make_async_copy(s_buf.at[j, pl.ds(2 * quarter, 2), :, half], r_buf.at[j, x], r_rs.at[j]).start()

    def g_target(j, i):
        zr = NZ * j + i // 4
        tx = 4 * half + 2 * c + i % 4 // 2
        tc = i % 2
        return zr, tx, tc, (zr == z) & (tx == x) & (tc == c)

    def g_copy(j, i):
        zr, tx, tc, _ = g_target(j, i)
        return pltpu.make_async_remote_copy(
            src_ref=g_out.at[zr, i % 4],
            dst_ref=g_in.at[z, quarter],
            send_sem=g_ss.at[j, i],
            recv_sem=g_rs,
            device_id=at(tx, tc, y, zr),
            device_id_type=MESH,
        )

    def g_send(j, i):
        zr, _, _, own = g_target(j, i)

        @pl.when(jnp.logical_not(own))
        def _():
            g_copy(j, i).start()

        @pl.when(own)
        def _():
            pltpu.make_async_copy(g_out.at[zr, i % 4], g_in.at[z, quarter], g_rs).start()

    def g_done(j, i):
        @pl.when(jnp.logical_not(g_target(j, i)[3]))
        def _():
            g_copy(j, i).wait_send()

    def w_own(t):
        return (4 * half + y % 4 == x) & (2 * quarter + t == y)

    def w_copy(j, t):
        return pltpu.make_async_remote_copy(
            src_ref=w_buf.at[j, t],
            dst_ref=e_buf.at[j, :, y // 4],
            send_sem=w_ss.at[j, t],
            recv_sem=e_rs.at[j],
            device_id=at(4 * half + y % 4, c, 2 * quarter + t, z),
            device_id_type=MESH,
        )

    def update(j):
        pltpu.make_async_copy(r_buf.at[j], r_buf.at[j], r_rs.at[j]).wait()
        for i in range(NZ):
            g = []
            for t in range(2):
                total = r_buf[j, 0, t, i].astype(F32)
                for n in range(1, 8):
                    total = total + r_buf[j, n, t, i].astype(F32)
                g.append(total)
            ws = [[], []]
            for xr in range(2):
                mixed = []
                for cr in range(2):
                    low = 8 * xr + 4 * cr
                    packed = jnp.concatenate([g[t][low : low + 4] for t in range(2)], axis=0)
                    g_out[NZ * j + i, 2 * xr + cr] = packed
                    mixed.append(q_in[NZ * j + i, xr, cr] - 1.33 * packed)
                for t in range(2):
                    ws[t] += [mixed[cr][4 * t : 4 * t + 4] for cr in range(2)]
            for t in range(2):
                w_buf[j, t, i] = jnp.concatenate(ws[t], axis=0).astype(BF16)
        for t in range(2):
            own = w_own(t)

            @pl.when(jnp.logical_not(own))
            def _():
                w_copy(j, t).start()

            @pl.when(own)
            def _():
                pltpu.make_async_copy(w_buf.at[j, t], e_buf.at[j, :, y // 4], e_rs.at[j]).start()

        loop(0, 4 * NZ, lambda i: g_send(j, i))

    def ag_copy(j, i):
        px = (x + 4 + (2 * (i % 2) - 1) * ((i + 1) // 2)) % 8
        return pltpu.make_async_remote_copy(
            src_ref=e_buf.at[j],
            dst_ref=out.at[pl.ds(NZ * j, NZ), :, quarter, half, c],
            send_sem=ag_ss.at[j, i],
            recv_sem=ag_rs.at[j],
            device_id=at(px, c, y, z),
            device_id_type=MESH,
        )

    def gather(j):
        pltpu.make_async_copy(e_buf.at[j], e_buf.at[j], e_rs.at[j]).wait()
        loop(0, 7, lambda i: ag_copy(j, i).start())
        pltpu.make_async_copy(e_buf.at[j], out.at[pl.ds(NZ * j, NZ), :, quarter, half, c], ag_rs.at[j]).start()

    def sibling(j):
        part = out.at[pl.ds(NZ * j, NZ), :, :, :, c]
        return pltpu.make_async_remote_copy(
            src_ref=part, dst_ref=part, send_sem=f_ss.at[j], recv_sem=f_rs.at[j],
            device_id=at(x, 1 - c, y, z), device_id_type=MESH,
        )

    def forward(j):
        part = out.at[pl.ds(NZ * j, NZ), :, :, :, c]
        pltpu.make_async_copy(part, part, ag_rs.at[j]).wait()
        sibling(j).start()

    for step in range(CHUNKS + 3):
        if step < CHUNKS:
            pltpu.make_async_copy(a_buf.at[step], a_buf.at[step], a_rs.at[step]).wait()
            if step + 2 < CHUNKS:
                send_y(step + 2)
            compute(step)
            send_x(step)
        if 0 <= step - 1 < CHUNKS:
            if step == 1:
                pltpu.make_async_copy(q_in, q_in, q_rs).wait()
            update(step - 1)
        if 0 <= step - 2 < CHUNKS:
            gather(step - 2)
        if step == CHUNKS + 1:
            pltpu.make_async_copy(g_in, g_in, g_rs).wait()
            for n in range(32):
                both = g_in[n // 4, n % 4]
                for t in range(2):
                    cols = slice((2 * n + t) * 128, (2 * n + t + 1) * 128)
                    g = both[4 * t : 4 * t + 4]
                    m = 0.9 * m_in[:, cols] + g
                    new_momentum[:, cols] = m
                    new_params[:, cols] = p_in[:, cols] - 0.7 * (g + 0.9 * m)
        if 0 <= step - 3 < CHUNKS:
            forward(step - 3)

    for j in range(CHUNKS):
        loop(0, 15, lambda i: y_copy(j, i).wait_send())
        loop(0, 7, lambda i: x_copy(j, i).wait_send())
        loop(0, 7, lambda i: ag_copy(j, i).wait_send())
        loop(0, 4 * NZ, lambda i: g_done(j, i))
        for t in range(2):

            @pl.when(jnp.logical_not(w_own(t)))
            def _():
                w_copy(j, t).wait_send()

    loop(0, 32, q_done)
    for j in range(CHUNKS):
        sibling(j).wait_send()
        part = out.at[pl.ds(NZ * j, NZ), :, :, :, 1 - c]
        pltpu.make_async_copy(part, part, f_rs.at[j]).wait()


def body(deltas, sign_bits, kept_tiles, kept_count, params, momentum):
    anywhere = pl.BlockSpec(memory_space=pl.ANY)
    vmem = pl.BlockSpec(memory_space=pltpu.VMEM)
    new_params, new_momentum, working = pl.pallas_call(
        kernel,
        out_shape=(
            jax.ShapeDtypeStruct(params.shape, F32),
            jax.ShapeDtypeStruct(params.shape, F32),
            jax.ShapeDtypeStruct((8, 2, 4, 2, 2, 16, 128), BF16),
        ),
        in_specs=[anywhere, anywhere, vmem, pl.BlockSpec(memory_space=pltpu.SMEM), anywhere, anywhere],
        out_specs=(vmem, vmem, anywhere),
        scratch_shapes=[
            pltpu.VMEM((CHUNKS, 8, 2, NZ, 2, 16, 128), BF16),
            pltpu.VMEM((CHUNKS, 8, NZ, 2, 16, 128), BF16),
            pltpu.VMEM((CHUNKS, 8, 2, NZ, 16, 128), BF16),
            pltpu.VMEM((CHUNKS, 2, NZ, 16, 128), BF16),
            pltpu.VMEM((CHUNKS, NZ, 2, 16, 128), BF16),
            pltpu.VMEM((8, 4, 8, 128), F32),
            pltpu.VMEM((8, 2, 2, 8, 128), F32),
            pltpu.VMEM((8, 4, 8, 128), F32),
            pltpu.VMEM((8, 4, 8, 128), F32),
            pltpu.VMEM((8, 1024), jnp.int32),
            pltpu.VMEM((2, 8, 128), F32),
            pltpu.VMEM((2, 8, 128), F32),
            pltpu.VMEM(params.shape, F32),
            pltpu.VMEM(params.shape, F32),
            DMA((CHUNKS, 15)),
            DMA((CHUNKS,)),
            DMA((CHUNKS, 7)),
            DMA((CHUNKS,)),
            DMA((CHUNKS, 2)),
            DMA((CHUNKS,)),
            DMA((CHUNKS, 7)),
            DMA((CHUNKS,)),
            DMA((CHUNKS,)),
            DMA((CHUNKS,)),
            DMA((32,)),
            DMA,
            DMA((CHUNKS, 4 * NZ)),
            DMA,
            DMA((3,)),
        ],
        compiler_params=pltpu.CompilerParams(
            collective_id=0, has_side_effects=True, vmem_limit_bytes=32 * 2**20
        ),
    )(deltas.reshape(8, 8, 2, 2, 16, 128), sign_bits, kept_tiles, kept_count, params, momentum)
    return new_params, new_momentum, working.reshape(4096, 128)


def solution(mesh):
    placed = (P("rep", None, "fsdp"), P(), P(), P(), P(("fsdp", "rep"), None), P(("fsdp", "rep"), None))
    return jax.shard_map(
        body,
        mesh=mesh,
        in_specs=placed,
        out_specs=(P(("fsdp", "rep"), None), P(("fsdp", "rep"), None), P(None, "fsdp")),
        check_vma=False,
    )
```

```python
import jax
import jax.numpy as jnp
from jax import lax
from jax.experimental import pallas as pl
from jax.experimental.pallas import tpu as pltpu
from jax.sharding import PartitionSpec as P

MESH = pl.DeviceIdType.MESH
DMA = pltpu.SemaphoreType.DMA
CHUNKS = 4
NZ = 8 // CHUNKS
MOST = 32
F32 = jnp.float32
BF16 = jnp.bfloat16


def place():
    rep = lax.axis_index("rep")
    col = lax.axis_index("fsdp")
    return rep >> 1, rep & 1, col & 7, col >> 3


def at(x, c, y, z):
    return (2 * x + c, 8 * z + y)


def loop(low, high, body):
    def step(i, carry):
        body(i)
        return carry

    lax.fori_loop(low, high, step, jnp.int32(0))


def butterfly(v):
    for bit in (1, 2, 4):
        v = [v[i] + v[i | bit] if not i & bit else v[i ^ bit] - v[i] for i in range(8)]
    return v


def hadamard128():
    i = lax.broadcasted_iota(jnp.int32, (128, 128), 0)
    j = lax.broadcasted_iota(jnp.int32, (128, 128), 1)
    v = i & j
    v = v ^ (v >> 4)
    v = v ^ (v >> 2)
    v = v ^ (v >> 1)
    return (1 - 2 * (v & 1)).astype(F32).astype(BF16)


def kernel(
    deltas, bits, tiles, counts, params, momentum,
    new_params, new_momentum, out,
    a_buf, s_buf, r_buf, w_buf, e_buf, full, q_out, q_in, g_out, g_in, sign_in, tiles_in, counts_in, signs, weights, p_in, m_in,
    a_ss, a_rs, r_ss, r_rs, w_ss, e_rs, ag_ss, ag_rs, f_ss, f_rs, q_ss, q_rs, g_ss, g_rs, l_sem,
):
    x, c, y, z = place()
    half = x >> 2
    quarter = x & 3
    pair = quarter >> 1

    loads = [
        pltpu.make_async_copy(bits.at[pl.ds(pl.multiple_of(half * 8, 8), 8), pl.ds(pl.multiple_of(z * 1024, 1024), 1024)], sign_in, l_sem.at[0]),
        pltpu.make_async_copy(params, p_in, l_sem.at[1]),
        pltpu.make_async_copy(momentum, m_in, l_sem.at[2]),
        pltpu.make_async_copy(tiles, tiles_in, l_sem.at[3]),
        pltpu.make_async_copy(counts, counts_in, l_sem.at[4]),
    ]
    for load in loads:
        load.start()

    barrier = pltpu.get_barrier_semaphore()

    def greet(device):
        pl.semaphore_signal(barrier, inc=1, device_id=device, device_id_type=MESH)

    def greet_y(i):
        p = (2 * y + c + i) & 15
        greet(at(x, p & 1, p >> 1, z))

    def greet_x(i):
        greet(at((x + i) & 7, c, y, z))

    def greet_z(i):
        p = (z * 8 + quarter * 2 + c + i) & 63
        greet(at(4 * half + ((p & 7) >> 1), p & 1, y, p >> 3))

    loop(1, 16, greet_y)
    loop(1, 8, greet_x)
    loop(1, 64, greet_z)
    stays = ((4 * half + (y & 3)) == x) & (((y >> 1)) == quarter)
    for t in range(2):
        own = (4 * half + (y & 3) == x) & (2 * quarter + t == y)

        @pl.when(jnp.logical_not(own))
        def _():
            greet(at(4 * half + (y & 3), c, 2 * quarter + t, z))

        own_in = (4 * half + (y >> 1) == x) & (quarter + 4 * t == y)

        @pl.when(jnp.logical_not(own_in))
        def _():
            greet(at(4 * half + (y >> 1), c, quarter + 4 * t, z))

    pl.semaphore_wait(barrier, 15 + 7 + 63 + 4 - 2 * stays.astype(jnp.int32))

    def y_peer(i):
        k = 8 + (2 * (i & 1) - 1) * ((i + 1) >> 1)
        p = (2 * y + c + k) & 15
        return p >> 1, p & 1

    def y_copy(j, i):
        py, pc = y_peer(i)
        return pltpu.make_async_remote_copy(
            src_ref=deltas.at[pl.ds(NZ * j, NZ), py, :, pc],
            dst_ref=a_buf.at[j, 2 * y + c],
            send_sem=a_ss.at[j],
            recv_sem=a_rs.at[j],
            device_id=at(x, pc, py, z),
            device_id_type=MESH,
        )

    def send_y(j):
        loop(0, 15, lambda i: y_copy(j, i).start())
        pltpu.make_async_copy(deltas.at[pl.ds(NZ * j, NZ), y, :, c], a_buf.at[j, 2 * y + c], a_rs.at[j]).start()

    send_y(0)

    loads[1].wait()
    loads[2].wait()
    for n in range(32):
        both = [
            p_in[:, (2 * n + t) * 128 : (2 * n + t + 1) * 128] - 0.567 * m_in[:, (2 * n + t) * 128 : (2 * n + t + 1) * 128]
            for t in range(2)
        ]
        q_out[n // 4, n % 4] = jnp.concatenate(both, axis=0)

    def q_target(i):
        pz = (z + (i >> 2)) & 7
        m = i & 3
        return pz, m, (4 * half + m == x) & (pair == c) & (pz == z)

    def q_copy(i):
        pz, m, _ = q_target(i)
        return pltpu.make_async_remote_copy(
            src_ref=q_out.at[pz, m],
            dst_ref=q_in.at[z, x & 1, c],
            send_sem=q_ss,
            recv_sem=q_rs,
            device_id=at(4 * half + m, pair, y, pz),
            device_id_type=MESH,
        )

    def q_send(i):
        pz, m, own = q_target(i)

        @pl.when(jnp.logical_not(own))
        def _():
            q_copy(i).start()

        @pl.when(own)
        def _():
            pltpu.make_async_copy(q_out.at[pz, m], q_in.at[z, x & 1, c], q_rs).start()

    loop(0, 32, q_send)
    for j in range(1, CHUNKS):
        send_y(j)

    loads[0].wait()
    loads[3].wait()
    loads[4].wait()
    lane = lax.broadcasted_iota(jnp.int32, (8, MOST), 1)
    wanted = lax.broadcasted_iota(jnp.int32, (8, MOST), 0) + 8 * z
    for s in range(2):
        row = sign_in[pl.ds(2 * quarter + s, 1), :]
        for k in range(8):
            signs[s, k : k + 1, :] = (1 - 2 * row[:, k * 128 : (k + 1) * 128]).astype(F32)
        count = counts_in[2 * x + s]
        kept = (tiles_in[pl.ds(2 * x + s, 1), :] == wanted) & (lane < count)
        mask = jnp.sum(kept.astype(F32), axis=1, keepdims=True)
        factor = (64.0 / 32.0) / jnp.full((8, 128), count, jnp.int32).astype(F32)
        weights[s] = mask * factor

    h128 = hadamard128()

    def rotate(parts):
        stacked = jnp.concatenate([parts[k][s] for k in range(8) for s in range(2)], axis=0)
        full = jnp.dot(stacked, h128, preferred_element_type=F32)
        return [[full[(2 * k + s) * 32 : (2 * k + s + 1) * 32] for s in range(2)] for k in range(8)]

    def columns(lists, f):
        sides = [f(s, [lists[k][s] for k in range(8)]) for s in range(2)]
        return [[sides[s][k] for s in range(2)] for k in range(8)]

    def compute(j):
        def group(i):
            flipped = [
                [(a_buf[j, 2 * k + s, i].reshape(32, 128).astype(F32) * signs[s, k : k + 1, :]).astype(BF16) for s in range(2)]
                for k in range(8)
            ]

            def middle(s, v):
                v = butterfly(v)
                return [(v[k] * weights[s, k : k + 1, :]).astype(BF16) for k in range(8)]

            def last(s, v):
                v = butterfly(v)
                return [v[k] * (signs[s, k : k + 1, :] * (1.0 / 512.0)) for k in range(8)]

            back = columns(rotate(columns(rotate(flipped), middle)), last)
            for k in range(8):
                both = (back[k][0] + back[k][1]).astype(BF16).reshape(2, 16, 128)
                for h in range(2):
                    s_buf[j, h, k, i] = both[h]

        loop(0, NZ, group)

    def x_copy(j, i):
        px = (x + 4 + (2 * (i & 1) - 1) * ((i + 1) >> 1)) & 7
        return pltpu.make_async_remote_copy(
            src_ref=s_buf.at[j, px >> 2, pl.ds(2 * (px & 3), 2)],
            dst_ref=r_buf.at[j, x],
            send_sem=r_ss.at[j],
            recv_sem=r_rs.at[j],
            device_id=at(px, c, y, z),
            device_id_type=MESH,
        )

    def send_x(j):
        loop(0, 7, lambda i: x_copy(j, i).start())
        pltpu.make_async_copy(s_buf.at[j, half, pl.ds(2 * quarter, 2)], r_buf.at[j, x], r_rs.at[j]).start()

    def g_target(j, i):
        zr = NZ * j + (i >> 2)
        tx = 4 * half + 2 * c + ((i & 3) >> 1)
        tc = i & 1
        return zr, tx, tc, (zr == z) & (tx == x) & (tc == c)

    def g_copy(j, i):
        zr, tx, tc, _ = g_target(j, i)
        return pltpu.make_async_remote_copy(
            src_ref=g_out.at[4 * zr + (i & 3)],
            dst_ref=g_in.at[z, quarter],
            send_sem=g_ss,
            recv_sem=g_rs,
            device_id=at(tx, tc, y, zr),
            device_id_type=MESH,
        )

    def g_send(j, i):
        zr, _, _, own = g_target(j, i)

        @pl.when(jnp.logical_not(own))
        def _():
            g_copy(j, i).start()

        @pl.when(own)
        def _():
            pltpu.make_async_copy(g_out.at[4 * zr + (i & 3)], g_in.at[z, quarter], g_rs).start()

    def w_own(t):
        return (4 * half + (y & 3) == x) & (2 * quarter + t == y)

    def w_copy(j, t):
        return pltpu.make_async_remote_copy(
            src_ref=w_buf.at[j, t],
            dst_ref=e_buf.at[j, y >> 2],
            send_sem=w_ss.at[j, t],
            recv_sem=e_rs.at[j],
            device_id=at(4 * half + (y & 3), c, 2 * quarter + t, z),
            device_id_type=MESH,
        )

    def update(j):
        pltpu.make_async_copy(r_buf.at[j], r_buf.at[j], r_rs.at[j]).wait()
        for i in range(NZ):
            g = []
            for t in range(2):
                total = r_buf[j, 0, t, i].astype(F32)
                for n in range(1, 8):
                    total = total + r_buf[j, n, t, i].astype(F32)
                g.append(total)
            ws = [[], []]
            for xr in range(2):
                mixed = []
                for cr in range(2):
                    low = 8 * xr + 4 * cr
                    packed = jnp.concatenate([g[t][low : low + 4] for t in range(2)], axis=0)
                    g_out[4 * (NZ * j + i) + 2 * xr + cr] = packed
                    mixed.append(q_in[NZ * j + i, xr, cr] - 1.33 * packed)
                for t in range(2):
                    ws[t] += [mixed[cr][4 * t : 4 * t + 4] for cr in range(2)]
            for t in range(2):
                w_buf[j, t, i] = jnp.concatenate(ws[t], axis=0).astype(BF16)
        for t in range(2):
            own = w_own(t)

            @pl.when(jnp.logical_not(own))
            def _():
                w_copy(j, t).start()

            @pl.when(own)
            def _():
                pltpu.make_async_copy(w_buf.at[j, t], e_buf.at[j, y >> 2], e_rs.at[j]).start()

        loop(0, 4 * NZ, lambda i: g_send(j, i))

    def ag_copy(j, i):
        px = (x + 4 + (2 * (i & 1) - 1) * ((i + 1) >> 1)) & 7
        return pltpu.make_async_remote_copy(
            src_ref=e_buf.at[j],
            dst_ref=full.at[j, c, x],
            send_sem=ag_ss.at[j],
            recv_sem=ag_rs.at[j],
            device_id=at(px, c, y, z),
            device_id_type=MESH,
        )

    def gather(j):
        pltpu.make_async_copy(e_buf.at[j], e_buf.at[j], e_rs.at[j]).wait()
        loop(0, 7, lambda i: ag_copy(j, i).start())
        pltpu.make_async_copy(e_buf.at[j], full.at[j, c, x], ag_rs.at[j]).start()

    def sibling(j):
        part = full.at[j, c]
        return pltpu.make_async_remote_copy(
            src_ref=part, dst_ref=part, send_sem=f_ss.at[j], recv_sem=f_rs.at[j],
            device_id=at(x, 1 - c, y, z), device_id_type=MESH,
        )

    def forward(j):
        part = full.at[j, c]
        pltpu.make_async_copy(part, part, ag_rs.at[j]).wait()
        sibling(j).start()

    def arrange(j, side):
        def one(n):
            for s in range(2):
                for i in range(NZ):
                    out[NZ * j + i, s, n & 3, n >> 2, side] = full[j, side, n, s, i]

        loop(0, 8, one)

    def finish(j):
        pltpu.make_async_copy(full.at[j, 1 - c], full.at[j, 1 - c], f_rs.at[j]).wait()
        arrange(j, 1 - c)

    for step in range(CHUNKS + 3):
        if step < CHUNKS:
            pltpu.make_async_copy(a_buf.at[step], a_buf.at[step], a_rs.at[step]).wait()
            compute(step)
            send_x(step)
        if 0 <= step - 1 < CHUNKS:
            if step == 1:
                pltpu.make_async_copy(q_in, q_in, q_rs).wait()
            update(step - 1)
        if 0 <= step - 2 < CHUNKS:
            gather(step - 2)
        if step == CHUNKS + 1:
            pltpu.make_async_copy(g_in, g_in, g_rs).wait()
            for n in range(32):
                both = g_in[n // 4, n % 4]
                for t in range(2):
                    cols = slice((2 * n + t) * 128, (2 * n + t + 1) * 128)
                    g = both[4 * t : 4 * t + 4]
                    m = 0.9 * m_in[:, cols] + g
                    new_momentum[:, cols] = m
                    new_params[:, cols] = p_in[:, cols] - 0.7 * (g + 0.9 * m)
        if 0 <= step - 3 < CHUNKS:
            forward(step - 3)
            arrange(step - 3, c)

    def drain(ref, sem):
        pltpu.make_async_copy(ref, ref, sem).wait()

    for j in range(CHUNKS):
        drain(a_buf.at[j, pl.ds(0, 15)], a_ss.at[j])
        drain(r_buf.at[j, pl.ds(0, 7)], r_ss.at[j])
        drain(r_buf.at[j, pl.ds(0, 7)], ag_ss.at[j])
        for t in range(2):

            @pl.when(jnp.logical_not(w_own(t)))
            def _():
                w_copy(j, t).wait_send()

    mine = pair == c

    @pl.when(mine)
    def _():
        drain(g_out.at[pl.ds(0, 31)], g_ss)
        drain(g_out.at[pl.ds(0, 31)], q_ss)

    @pl.when(jnp.logical_not(mine))
    def _():
        drain(g_out, g_ss)
        drain(g_out, q_ss)

    for j in range(CHUNKS):
        sibling(j).wait_send()
        finish(j)


def body(deltas, sign_bits, kept_tiles, kept_count, params, momentum):
    anywhere = pl.BlockSpec(memory_space=pl.ANY)
    vmem = pl.BlockSpec(memory_space=pltpu.VMEM)
    new_params, new_momentum, working = pl.pallas_call(
        kernel,
        out_shape=(
            jax.ShapeDtypeStruct(params.shape, F32),
            jax.ShapeDtypeStruct(params.shape, F32),
            jax.ShapeDtypeStruct((8, 2, 4, 2, 2, 16, 128), BF16),
        ),
        in_specs=[anywhere] * 6,
        out_specs=(vmem, vmem, vmem),
        scratch_shapes=[
            pltpu.VMEM((CHUNKS, 16, NZ, 2, 16, 128), BF16),
            pltpu.VMEM((CHUNKS, 2, 8, NZ, 16, 128), BF16),
            pltpu.VMEM((CHUNKS, 8, 2, NZ, 16, 128), BF16),
            pltpu.VMEM((CHUNKS, 2, NZ, 16, 128), BF16),
            pltpu.VMEM((CHUNKS, 2, NZ, 16, 128), BF16),
            pltpu.VMEM((CHUNKS, 2, 8, 2, NZ, 16, 128), BF16),
            pltpu.VMEM((8, 4, 8, 128), F32),
            pltpu.VMEM((8, 2, 2, 8, 128), F32),
            pltpu.VMEM((32, 8, 128), F32),
            pltpu.VMEM((8, 4, 8, 128), F32),
            pltpu.VMEM((8, 1024), jnp.int32),
            pltpu.VMEM((16, MOST), jnp.int32),
            pltpu.SMEM((16,), jnp.int32),
            pltpu.VMEM((2, 8, 128), F32),
            pltpu.VMEM((2, 8, 128), F32),
            pltpu.VMEM(params.shape, F32),
            pltpu.VMEM(params.shape, F32),
            DMA((CHUNKS,)),
            DMA((CHUNKS,)),
            DMA((CHUNKS,)),
            DMA((CHUNKS,)),
            DMA((CHUNKS, 2)),
            DMA((CHUNKS,)),
            DMA((CHUNKS,)),
            DMA((CHUNKS,)),
            DMA((CHUNKS,)),
            DMA((CHUNKS,)),
            DMA,
            DMA,
            DMA,
            DMA,
            DMA((5,)),
        ],
        compiler_params=pltpu.CompilerParams(
            collective_id=0, has_side_effects=True, vmem_limit_bytes=60 * 2**20
        ),
    )(deltas.reshape(8, 8, 2, 2, 16, 128), sign_bits, kept_tiles, kept_count, params, momentum)
    return new_params, new_momentum, working.reshape(4096, 128)


def solution(mesh):
    placed = (P("rep", None, "fsdp"), P(), P(), P(), P(("fsdp", "rep"), None), P(("fsdp", "rep"), None))
    return jax.shard_map(
        body,
        mesh=mesh,
        in_specs=placed,
        out_specs=(P(("fsdp", "rep"), None), P(("fsdp", "rep"), None), P(None, "fsdp")),
        check_vma=False,
    )
```

```python
import jax
import jax.numpy as jnp
from jax import lax
from jax.experimental import pallas as pl
from jax.experimental.pallas import tpu as pltpu
from jax.sharding import PartitionSpec as P

MESH = pl.DeviceIdType.MESH
DMA = pltpu.SemaphoreType.DMA
CHUNKS = 2
NZ = 8 // CHUNKS
MOST = 32
F32 = jnp.float32
BF16 = jnp.bfloat16


def place():
    rep = lax.axis_index("rep")
    col = lax.axis_index("fsdp")
    return rep >> 1, rep & 1, col & 7, col >> 3


def at(x, c, y, z):
    return (2 * x + c, 8 * z + y)


def loop(low, high, body):
    def step(i, carry):
        body(i)
        return carry

    lax.fori_loop(low, high, step, jnp.int32(0))


def butterfly(v):
    for bit in (1, 2, 4):
        v = [v[i] + v[i | bit] if not i & bit else v[i ^ bit] - v[i] for i in range(8)]
    return v


def hadamard128():
    i = lax.broadcasted_iota(jnp.int32, (128, 128), 0)
    j = lax.broadcasted_iota(jnp.int32, (128, 128), 1)
    v = i & j
    v = v ^ (v >> 4)
    v = v ^ (v >> 2)
    v = v ^ (v >> 1)
    return (1 - 2 * (v & 1)).astype(F32).astype(BF16)


def kernel(
    deltas, bits, tiles, counts, params, momentum,
    new_params, new_momentum, out,
    a_buf, s_buf, r_buf, w_buf, e_buf, full, q_out, q_in, g_out, g_in, sign_in, tiles_in, counts_in, signs, weights, p_in, m_in,
    a_ss, a_rs, r_ss, r_rs, w_ss, e_rs, ag_ss, ag_rs, f_ss, f_rs, q_ss, q_rs, g_ss, g_rs, l_sem,
):
    x, c, y, z = place()
    half = x >> 2
    quarter = x & 3
    pair = quarter >> 1

    loads = [
        pltpu.make_async_copy(bits.at[pl.ds(pl.multiple_of(half * 8, 8), 8), pl.ds(pl.multiple_of(z * 1024, 1024), 1024)], sign_in, l_sem.at[0]),
        pltpu.make_async_copy(params, p_in, l_sem.at[1]),
        pltpu.make_async_copy(momentum, m_in, l_sem.at[2]),
        pltpu.make_async_copy(tiles, tiles_in, l_sem.at[3]),
        pltpu.make_async_copy(counts, counts_in, l_sem.at[4]),
    ]
    for load in loads:
        load.start()

    barrier = pltpu.get_barrier_semaphore()

    def greet(device):
        pl.semaphore_signal(barrier, inc=1, device_id=device, device_id_type=MESH)

    def greet_y(i):
        p = (2 * y + c + i) & 15
        greet(at(x, p & 1, p >> 1, z))

    def greet_x(i):
        greet(at((x + i) & 7, c, y, z))

    def greet_z(i):
        p = (z * 8 + quarter * 2 + c + i) & 63
        greet(at(4 * half + ((p & 7) >> 1), p & 1, y, p >> 3))

    loop(1, 16, greet_y)
    loop(1, 8, greet_x)
    loop(1, 64, greet_z)
    stays = ((4 * half + (y & 3)) == x) & (((y >> 1)) == quarter)
    for t in range(2):
        own = (4 * half + (y & 3) == x) & (2 * quarter + t == y)

        @pl.when(jnp.logical_not(own))
        def _():
            greet(at(4 * half + (y & 3), c, 2 * quarter + t, z))

        own_in = (4 * half + (y >> 1) == x) & (quarter + 4 * t == y)

        @pl.when(jnp.logical_not(own_in))
        def _():
            greet(at(4 * half + (y >> 1), c, quarter + 4 * t, z))

    pl.semaphore_wait(barrier, 15 + 7 + 63 + 4 - 2 * stays.astype(jnp.int32))

    def y_peer(i):
        k = 8 + (2 * (i & 1) - 1) * ((i + 1) >> 1)
        p = (2 * y + c + k) & 15
        return p >> 1, p & 1

    def y_copy(j, i):
        py, pc = y_peer(i)
        return pltpu.make_async_remote_copy(
            src_ref=deltas.at[pl.ds(NZ * j, NZ), py, :, pc],
            dst_ref=a_buf.at[j, 2 * y + c],
            send_sem=a_ss.at[j],
            recv_sem=a_rs.at[j],
            device_id=at(x, pc, py, z),
            device_id_type=MESH,
        )

    def send_y(j):
        loop(0, 15, lambda i: y_copy(j, i).start())
        pltpu.make_async_copy(deltas.at[pl.ds(NZ * j, NZ), y, :, c], a_buf.at[j, 2 * y + c], a_rs.at[j]).start()

    send_y(0)

    loads[1].wait()
    loads[2].wait()
    for n in range(32):
        both = [
            p_in[:, (2 * n + t) * 128 : (2 * n + t + 1) * 128] - 0.567 * m_in[:, (2 * n + t) * 128 : (2 * n + t + 1) * 128]
            for t in range(2)
        ]
        q_out[n // 4, n % 4] = jnp.concatenate(both, axis=0)

    def q_target(i):
        pz = (z + (i >> 2)) & 7
        m = i & 3
        return pz, m, (4 * half + m == x) & (pair == c) & (pz == z)

    def q_copy(i):
        pz, m, _ = q_target(i)
        return pltpu.make_async_remote_copy(
            src_ref=q_out.at[pz, m],
            dst_ref=q_in.at[z, x & 1, c],
            send_sem=q_ss,
            recv_sem=q_rs,
            device_id=at(4 * half + m, pair, y, pz),
            device_id_type=MESH,
        )

    def q_send(i):
        pz, m, own = q_target(i)

        @pl.when(jnp.logical_not(own))
        def _():
            q_copy(i).start()

        @pl.when(own)
        def _():
            pltpu.make_async_copy(q_out.at[pz, m], q_in.at[z, x & 1, c], q_rs).start()

    loop(0, 32, q_send)
    for j in range(1, CHUNKS):
        send_y(j)

    loads[0].wait()
    loads[3].wait()
    loads[4].wait()
    lane = lax.broadcasted_iota(jnp.int32, (8, MOST), 1)
    wanted = lax.broadcasted_iota(jnp.int32, (8, MOST), 0) + 8 * z
    for s in range(2):
        row = sign_in[pl.ds(2 * quarter + s, 1), :]
        for k in range(8):
            signs[s, k : k + 1, :] = (1 - 2 * row[:, k * 128 : (k + 1) * 128]).astype(F32)
        count = counts_in[2 * x + s]
        kept = (tiles_in[pl.ds(2 * x + s, 1), :] == wanted) & (lane < count)
        mask = jnp.sum(kept.astype(F32), axis=1, keepdims=True)
        factor = (64.0 / 32.0) / jnp.full((8, 128), count, jnp.int32).astype(F32)
        weights[s] = mask * factor

    h128 = hadamard128()

    def rotate(parts):
        stacked = jnp.concatenate([parts[k][s] for k in range(8) for s in range(2)], axis=0)
        full = jnp.dot(stacked, h128, preferred_element_type=F32)
        return [[full[(2 * k + s) * 32 : (2 * k + s + 1) * 32] for s in range(2)] for k in range(8)]

    def columns(lists, f):
        sides = [f(s, [lists[k][s] for k in range(8)]) for s in range(2)]
        return [[sides[s][k] for s in range(2)] for k in range(8)]

    def compute(j):
        def group(i):
            flipped = [
                [(a_buf[j, 2 * k + s, i].reshape(32, 128).astype(F32) * signs[s, k : k + 1, :]).astype(BF16) for s in range(2)]
                for k in range(8)
            ]

            def middle(s, v):
                v = butterfly(v)
                return [(v[k] * weights[s, k : k + 1, :]).astype(BF16) for k in range(8)]

            def last(s, v):
                v = butterfly(v)
                return [v[k] * (signs[s, k : k + 1, :] * (1.0 / 512.0)) for k in range(8)]

            back = columns(rotate(columns(rotate(flipped), middle)), last)
            for k in range(8):
                both = (back[k][0] + back[k][1]).astype(BF16).reshape(2, 16, 128)
                for h in range(2):
                    s_buf[j, h, k, i] = both[h]

        loop(0, NZ, group)

    def x_copy(j, i):
        px = (x + 4 + (2 * (i & 1) - 1) * ((i + 1) >> 1)) & 7
        return pltpu.make_async_remote_copy(
            src_ref=s_buf.at[j, px >> 2, pl.ds(2 * (px & 3), 2)],
            dst_ref=r_buf.at[j, x],
            send_sem=r_ss.at[j],
            recv_sem=r_rs.at[j],
            device_id=at(px, c, y, z),
            device_id_type=MESH,
        )

    def send_x(j):
        loop(0, 7, lambda i: x_copy(j, i).start())
        pltpu.make_async_copy(s_buf.at[j, half, pl.ds(2 * quarter, 2)], r_buf.at[j, x], r_rs.at[j]).start()

    def g_target(j, i):
        zr = NZ * j + (i >> 2)
        tx = 4 * half + 2 * c + ((i & 3) >> 1)
        tc = i & 1
        return zr, tx, tc, (zr == z) & (tx == x) & (tc == c)

    def g_copy(j, i):
        zr, tx, tc, _ = g_target(j, i)
        return pltpu.make_async_remote_copy(
            src_ref=g_out.at[4 * zr + (i & 3)],
            dst_ref=g_in.at[z, quarter],
            send_sem=g_ss,
            recv_sem=g_rs,
            device_id=at(tx, tc, y, zr),
            device_id_type=MESH,
        )

    def g_send(j, i):
        zr, _, _, own = g_target(j, i)

        @pl.when(jnp.logical_not(own))
        def _():
            g_copy(j, i).start()

        @pl.when(own)
        def _():
            pltpu.make_async_copy(g_out.at[4 * zr + (i & 3)], g_in.at[z, quarter], g_rs).start()

    def w_own(t):
        return (4 * half + (y & 3) == x) & (2 * quarter + t == y)

    def w_copy(j, t):
        return pltpu.make_async_remote_copy(
            src_ref=w_buf.at[j, t],
            dst_ref=e_buf.at[j, y >> 2],
            send_sem=w_ss.at[j, t],
            recv_sem=e_rs.at[j],
            device_id=at(4 * half + (y & 3), c, 2 * quarter + t, z),
            device_id_type=MESH,
        )

    def update(j):
        pltpu.make_async_copy(r_buf.at[j], r_buf.at[j], r_rs.at[j]).wait()
        for i in range(NZ):
            g = []
            for t in range(2):
                total = r_buf[j, 0, t, i].astype(F32)
                for n in range(1, 8):
                    total = total + r_buf[j, n, t, i].astype(F32)
                g.append(total)
            ws = [[], []]
            for xr in range(2):
                mixed = []
                for cr in range(2):
                    low = 8 * xr + 4 * cr
                    packed = jnp.concatenate([g[t][low : low + 4] for t in range(2)], axis=0)
                    g_out[4 * (NZ * j + i) + 2 * xr + cr] = packed
                    mixed.append(q_in[NZ * j + i, xr, cr] - 1.33 * packed)
                for t in range(2):
                    ws[t] += [mixed[cr][4 * t : 4 * t + 4] for cr in range(2)]
            for t in range(2):
                w_buf[j, t, i] = jnp.concatenate(ws[t], axis=0).astype(BF16)
        for t in range(2):
            own = w_own(t)

            @pl.when(jnp.logical_not(own))
            def _():
                w_copy(j, t).start()

            @pl.when(own)
            def _():
                pltpu.make_async_copy(w_buf.at[j, t], e_buf.at[j, y >> 2], e_rs.at[j]).start()

        loop(0, 4 * NZ, lambda i: g_send(j, i))

    def ag_copy(j, i):
        px = (x + 4 + (2 * (i & 1) - 1) * ((i + 1) >> 1)) & 7
        return pltpu.make_async_remote_copy(
            src_ref=e_buf.at[j],
            dst_ref=full.at[j, c, x],
            send_sem=ag_ss.at[j],
            recv_sem=ag_rs.at[j],
            device_id=at(px, c, y, z),
            device_id_type=MESH,
        )

    def gather(j):
        pltpu.make_async_copy(e_buf.at[j], e_buf.at[j], e_rs.at[j]).wait()
        loop(0, 7, lambda i: ag_copy(j, i).start())
        pltpu.make_async_copy(e_buf.at[j], full.at[j, c, x], ag_rs.at[j]).start()

    def sibling(j):
        part = full.at[j, c]
        return pltpu.make_async_remote_copy(
            src_ref=part, dst_ref=part, send_sem=f_ss.at[j], recv_sem=f_rs.at[j],
            device_id=at(x, 1 - c, y, z), device_id_type=MESH,
        )

    def forward(j):
        part = full.at[j, c]
        pltpu.make_async_copy(part, part, ag_rs.at[j]).wait()
        sibling(j).start()

    def arrange(j, side):
        def one(n):
            for s in range(2):
                for i in range(NZ):
                    out[NZ * j + i, s, n & 3, n >> 2, side] = full[j, side, n, s, i]

        loop(0, 8, one)

    def finish(j):
        pltpu.make_async_copy(full.at[j, 1 - c], full.at[j, 1 - c], f_rs.at[j]).wait()
        arrange(j, 1 - c)

    for step in range(CHUNKS + 3):
        if step < CHUNKS:
            pltpu.make_async_copy(a_buf.at[step], a_buf.at[step], a_rs.at[step]).wait()
            compute(step)
            send_x(step)
        if 0 <= step - 1 < CHUNKS:
            if step == 1:
                pltpu.make_async_copy(q_in, q_in, q_rs).wait()
            update(step - 1)
        if 0 <= step - 2 < CHUNKS:
            gather(step - 2)
        if step == CHUNKS + 1:
            pltpu.make_async_copy(g_in, g_in, g_rs).wait()
            for n in range(32):
                both = g_in[n // 4, n % 4]
                for t in range(2):
                    cols = slice((2 * n + t) * 128, (2 * n + t + 1) * 128)
                    g = both[4 * t : 4 * t + 4]
                    m = 0.9 * m_in[:, cols] + g
                    new_momentum[:, cols] = m
                    new_params[:, cols] = p_in[:, cols] - 0.7 * (g + 0.9 * m)
        if 0 <= step - 3 < CHUNKS:
            forward(step - 3)
            arrange(step - 3, c)

    def drain(ref, sem):
        pltpu.make_async_copy(ref, ref, sem).wait()

    for j in range(CHUNKS):
        drain(a_buf.at[j, pl.ds(0, 15)], a_ss.at[j])
        drain(r_buf.at[j, pl.ds(0, 7)], r_ss.at[j])
        drain(r_buf.at[j, pl.ds(0, 7)], ag_ss.at[j])
        for t in range(2):

            @pl.when(jnp.logical_not(w_own(t)))
            def _():
                w_copy(j, t).wait_send()

    mine = pair == c

    @pl.when(mine)
    def _():
        drain(g_out.at[pl.ds(0, 31)], g_ss)
        drain(g_out.at[pl.ds(0, 31)], q_ss)

    @pl.when(jnp.logical_not(mine))
    def _():
        drain(g_out, g_ss)
        drain(g_out, q_ss)

    for j in range(CHUNKS):
        sibling(j).wait_send()
        finish(j)


def body(deltas, sign_bits, kept_tiles, kept_count, params, momentum):
    anywhere = pl.BlockSpec(memory_space=pl.ANY)
    vmem = pl.BlockSpec(memory_space=pltpu.VMEM)
    new_params, new_momentum, working = pl.pallas_call(
        kernel,
        out_shape=(
            jax.ShapeDtypeStruct(params.shape, F32),
            jax.ShapeDtypeStruct(params.shape, F32),
            jax.ShapeDtypeStruct((8, 2, 4, 2, 2, 16, 128), BF16),
        ),
        in_specs=[anywhere] * 6,
        out_specs=(vmem, vmem, vmem),
        scratch_shapes=[
            pltpu.VMEM((CHUNKS, 16, NZ, 2, 16, 128), BF16),
            pltpu.VMEM((CHUNKS, 2, 8, NZ, 16, 128), BF16),
            pltpu.VMEM((CHUNKS, 8, 2, NZ, 16, 128), BF16),
            pltpu.VMEM((CHUNKS, 2, NZ, 16, 128), BF16),
            pltpu.VMEM((CHUNKS, 2, NZ, 16, 128), BF16),
            pltpu.VMEM((CHUNKS, 2, 8, 2, NZ, 16, 128), BF16),
            pltpu.VMEM((8, 4, 8, 128), F32),
            pltpu.VMEM((8, 2, 2, 8, 128), F32),
            pltpu.VMEM((32, 8, 128), F32),
            pltpu.VMEM((8, 4, 8, 128), F32),
            pltpu.VMEM((8, 1024), jnp.int32),
            pltpu.VMEM((16, MOST), jnp.int32),
            pltpu.SMEM((16,), jnp.int32),
            pltpu.VMEM((2, 8, 128), F32),
            pltpu.VMEM((2, 8, 128), F32),
            pltpu.VMEM(params.shape, F32),
            pltpu.VMEM(params.shape, F32),
            DMA((CHUNKS,)),
            DMA((CHUNKS,)),
            DMA((CHUNKS,)),
            DMA((CHUNKS,)),
            DMA((CHUNKS, 2)),
            DMA((CHUNKS,)),
            DMA((CHUNKS,)),
            DMA((CHUNKS,)),
            DMA((CHUNKS,)),
            DMA((CHUNKS,)),
            DMA,
            DMA,
            DMA,
            DMA,
            DMA((5,)),
        ],
        compiler_params=pltpu.CompilerParams(
            collective_id=0, has_side_effects=True, vmem_limit_bytes=60 * 2**20
        ),
    )(deltas.reshape(8, 8, 2, 2, 16, 128), sign_bits, kept_tiles, kept_count, params, momentum)
    return new_params, new_momentum, working.reshape(4096, 128)


def solution(mesh):
    placed = (P("rep", None, "fsdp"), P(), P(), P(), P(("fsdp", "rep"), None), P(("fsdp", "rep"), None))
    return jax.shard_map(
        body,
        mesh=mesh,
        in_specs=placed,
        out_specs=(P(("fsdp", "rep"), None), P(("fsdp", "rep"), None), P(None, "fsdp")),
        check_vma=False,
    )
```
